32 devices in a mesh: freq: 4 (over y, core), tri: 8 (over z, x).
Axes of the slice: x: 2, y: 2, z: 4, core: 2. Of those that a mesh axis runs over, the one named last changes fastest.
Arguments:
- voltages: int32 [2, 8, 256, 66304], P(None, 'tri', 'freq'), may hold values from -8 to 7
- window_taps: float32 [4, 256], replicated, may hold values from -3 to 3
Outputs:
- visibility: bfloat16 [128, 8, 5, 256, 2, 256], P('freq', 'tri')
The draws below stay inside these ranges and needn't reach their ends.
All inputs are finite; a program needn't handle non-finite values.
Results may differ from the reference program's by a relative error of at most 0.0055.
Values may be sent and summed in bfloat16 or wider, within the bound.
No kernel may reach another device: no remote copies, remote signals or barrier semaphores. Data moves between devices by JAX's collectives and lax.ppermute only.
A program may use at most 384 MiB of HBM per device.

```python
import math
import jax
import jax.numpy as jnp
from jax import lax

POINTS = 256
CHAN = 128
TAPS = 4
SPEC = 256
NBLK = 8
BLK = 256
HALF = 4
SAMP = 66304


def place_ends(drawn, key, smallest, high):
    longest = drawn.shape.index(max(drawn.shape))
    spots = []
    for shift in (0, 1):
        where = [jax.random.randint(jax.random.fold_in(key, axis), (), 0, length) for axis, length in enumerate(drawn.shape)]
        where[longest] = (where[longest] + shift) % drawn.shape[longest]
        spots.append(tuple(where))
    return drawn.at[spots[0]].set(smallest).at[spots[1]].set(high)


def bell_draw(stream_key, dims, scale, limit, kind=jnp.bfloat16):
    return jnp.clip(scale * jax.random.normal(stream_key, dims, jnp.float32), -limit, limit).astype(kind)


def setup_inputs(seed: int = 0) -> dict:
    splits = jax.random.split(jax.random.key(seed), 3)
    return {
        "voltages": place_ends(jax.random.randint(splits[0], (2, NBLK, BLK, SAMP), -8, 8), jax.random.fold_in(splits[0], 1), -8, 7).astype(jnp.int32),
        "window_taps": bell_draw(splits[1], (TAPS, POINTS), TAPS ** -0.5, 3.0, jnp.float32),
    }


spectrum_scale = 1.0 / 128.0


def fourier_table(points, chans):
    point_index = jnp.arange(points, dtype=jnp.int32)[:, None]
    chan_index = jnp.arange(chans, dtype=jnp.int32)[None, :]
    phase = ((point_index * chan_index) % points).astype(jnp.float32) * (2.0 * math.pi / points)
    cosine = jnp.cos(phase)
    sine = jnp.sin(phase)
    table = jnp.stack([jnp.stack([cosine, -sine], -1), jnp.stack([sine, cosine], -1)], 0)
    return table * spectrum_scale


def fir_frames(samples, window_taps, count):
    frames = samples[:, :, 0:count, :] * window_taps[0]
    for tap_index in range(1, window_taps.shape[0]):
        frames = frames + samples[:, :, tap_index:tap_index + count, :] * window_taps[tap_index]
    return frames


def cross_tile(left_rows, right_block):
    real_part = right_block[..., 0, :]
    imag_part = right_block[..., 1, :]
    stacked = jnp.stack([jnp.concatenate([real_part, imag_part], -1), jnp.concatenate([-imag_part, real_part], -1)], axis=-3)
    product = jnp.einsum("...at,...nbt->...anb", left_rows.astype(jnp.float32), stacked.astype(jnp.float32))
    return (product * (1.0 / SPEC)).astype(jnp.bfloat16)


def reference(voltages, window_taps):
    table = fourier_table(POINTS, CHAN)

    def channelize(block_index):
        block_volts = lax.dynamic_index_in_dim(voltages, block_index, 1, keepdims=False)
        samples = block_volts.reshape(2, BLK, SPEC + TAPS - 1, POINTS).astype(jnp.float32)
        frames = fir_frames(samples, window_taps, SPEC)
        result = jnp.einsum("qpcr,qimp->cirm", table, frames, precision=lax.Precision.HIGHEST)
        return result.astype(jnp.bfloat16)

    spectra = lax.map(channelize, jnp.arange(NBLK, dtype=jnp.int32))
    spectra = jnp.moveaxis(spectra, 1, 0)

    def correlate(chan_spectra):
        left_rows = chan_spectra.reshape(NBLK, BLK, 2 * SPEC)
        tile_list = [cross_tile(left_rows, jnp.roll(chan_spectra, -offset, axis=0)) for offset in range(HALF + 1)]
        return jnp.stack(tile_list, axis=1)

    return lax.map(correlate, spectra)
```

```python
import functools
import math

import jax
import jax.numpy as jnp
import numpy as np
from jax import lax
from jax.experimental import pallas as pl
from jax.experimental.pallas import tpu as pltpu
from jax.sharding import PartitionSpec as P

CHAN = 128


spectrum_scale = 1.0 / 128.0

LANES = 128
CHUNKS = (8, 8, 8, 8)
ROWS_EACH = ((((1,), (1,)), ((), ())))


def passed_along(value, axis, steps):
    count = lax.axis_size(axis)
    pairs = [(source, (source + steps) % count) for source in range(count)]
    return lax.ppermute(value, axis, pairs)


def fourier_table(points, chans):
    point_index = jnp.arange(points, dtype=jnp.int32)[:, None]
    chan_index = jnp.arange(chans, dtype=jnp.int32)[None, :]
    phase = (point_index * chan_index % points).astype(jnp.float32) * (2.0 * math.pi / points)
    cosine = jnp.cos(phase)
    sine = jnp.sin(phase)
    table = jnp.stack([jnp.stack([cosine, -sine], -1), jnp.stack([sine, cosine], -1)], 0)
    return table * spectrum_scale


def fir_frames(samples, window_taps, count):
    frames = samples[:, :, 0:count, :] * window_taps[0]
    for tap_index in range(1, window_taps.shape[0]):
        frames = frames + samples[:, :, tap_index : tap_index + count, :] * window_taps[tap_index]
    return frames


def cross_tile(left_rows, right_block):
    spectra_len = right_block.shape[-1]
    real_part = right_block[..., 0, :]
    imag_part = right_block[..., 1, :]
    stacked = jnp.stack(
        [jnp.concatenate([real_part, imag_part], -1), jnp.concatenate([-imag_part, real_part], -1)],
        axis=-3,
    )
    product = jnp.einsum(
        "...at,...nbt->...anb", left_rows, stacked, preferred_element_type=jnp.float32
    )
    return (product * (1.0 / spectra_len)).astype(jnp.bfloat16)


def on_device_any(voltages, window_taps):
    taps_count, points = window_taps.shape
    in_dev = voltages.shape[2]
    frames_total = voltages.shape[3] // points
    spectra_len = frames_total - taps_count + 1
    samples = voltages.reshape(2, in_dev, frames_total, points).astype(jnp.float32)
    frames = fir_frames(samples, window_taps, spectra_len)
    spectra = jnp.einsum(
        "qpcr,qimp->cirm", fourier_table(points, CHAN), frames, precision=lax.Precision.HIGHEST
    ).astype(jnp.bfloat16)
    half_count = lax.axis_size("tri") // 2
    own_block = lax.all_to_all(spectra, "freq", split_axis=0, concat_axis=1, tiled=True)
    group_chans, block_len = own_block.shape[:2]
    left_rows = own_block.reshape(group_chans, block_len, 2 * spectra_len)
    held = own_block[None]
    while held.shape[0] < half_count + 1:
        run_len = held.shape[0]
        count = min(run_len, half_count + 1 - run_len)
        received = passed_along(held[:count], "tri", -run_len)
        held = jnp.concatenate([held, received], 0)
    tile_list = [cross_tile(left_rows, held[offset]) for offset in range(half_count + 1)]
    return jnp.stack(tile_list, axis=1)[:, None]


def table_rows(points, chans):
    phase = (np.arange(points)[:, None] * np.arange(chans)[None, :] % points).astype(np.float64)
    phase = phase * (2.0 * math.pi / points)
    cosine, sine = np.cos(phase), np.sin(phase)
    real_row = np.concatenate([cosine, sine], 0).T
    imag_row = np.concatenate([-sine, cosine], 0).T
    return (np.stack([real_row, imag_row], 0) * spectrum_scale).astype(np.float32)


def channelize_kernel(chunks, spectra_len, volt_ref, taps_ref, table_ref, *refs):
    n_out = 3 * len(chunks)
    outs = refs[:n_out]
    frames_ref, spec_ref = refs[n_out:]
    points = taps_ref.shape[1]
    taps_count = taps_ref.shape[0] // 8
    lane_parts = points // LANES
    group = volt_ref.shape[2]
    total_chans = table_ref.shape[0] // 4
    n_rows = 2 * total_chans

    for sub in range(group // 8):
        for q in range(2):
            for part in range(lane_parts):
                weight = [
                    taps_ref[8 * k : 8 * k + 8, part * LANES : (part + 1) * LANES]
                    for k in range(taps_count)
                ]

                def sample(m, q=q, part=part, sub=sub):
                    start = pl.multiple_of(m * points + part * LANES, LANES)
                    return volt_ref[q, 0, 8 * sub : 8 * sub + 8, pl.ds(start, LANES)].astype(jnp.float32)

                step = 8

                def body(i, carry, weight=weight, sample=sample, q=q, part=part):
                    held = list(carry)
                    for r in range(step):
                        m = i * step + r
                        held.append(sample(m + taps_count - 1))
                        total = held[0] * weight[0]
                        for k in range(1, taps_count):
                            total = total + held[k] * weight[k]
                        held = held[1:]
                        row = pl.multiple_of(m * 8, 8)
                        frames_ref[q * lane_parts + part, pl.ds(row, 8), :] = total
                    return tuple(held)

                lax.fori_loop(
                    0, spectra_len // step, body, tuple(sample(k) for k in range(taps_count - 1))
                )

        def one_input(n, carry, sub=sub):
            frame = jnp.concatenate(
                [
                    frames_ref[part, pl.ds(n, spectra_len, stride=8), :]
                    for part in range(2 * lane_parts)
                ],
                axis=1,
            )
            high = frame.astype(jnp.bfloat16)
            low = (frame - high.astype(jnp.float32)).astype(jnp.bfloat16)
            first = lax.dot_general(
                table_ref[0 : 2 * n_rows, :], high, ROWS_EACH, preferred_element_type=jnp.float32
            )
            second = lax.dot_general(
                table_ref[0:n_rows, :], low, ROWS_EACH, preferred_element_type=jnp.float32
            )
            spec = first[:n_rows] + (first[n_rows:] + second)
            for ri in range(2):
                for part in range(spectra_len // LANES):
                    spec_ref[
                        ri * (spectra_len // LANES) + part,
                        pl.ds(sub * 8 + n, total_chans, stride=group),
                        :,
                    ] = spec[
                        ri * total_chans : (ri + 1) * total_chans, part * LANES : (part + 1) * LANES
                    ]
            return carry

        lax.fori_loop(0, 8, one_input, 0)

    group_chans = sum(chunks)
    n_parts = 2 * spectra_len // LANES
    start = 0
    for k, count in enumerate(chunks):
        near, across, paired = outs[3 * k : 3 * k + 3]
        for j, target in ((0, near), (2, across), (1, paired.at[0]), (3, paired.at[1])):
            base = (j * group_chans + start) * group
            for part in range(n_parts):
                piece = spec_ref[part, base : base + count * group, :].astype(jnp.bfloat16)
                target[:, :, part * LANES : (part + 1) * LANES] = piece.reshape(count, group, LANES)
        start += count


def channelize(voltages, window_taps, table, chunks):
    taps_count, points = window_taps.shape
    in_dev, samples = voltages.shape[2:]
    spectra_len = samples // points - taps_count + 1
    group = 16
    wide = 2 * spectra_len
    chans = table.shape[0] // 4
    taps = jnp.repeat(window_taps, 8, axis=0)
    shapes, specs = [], []
    for count in chunks:
        for lead in ((), (), (2,)):
            shapes.append(jax.ShapeDtypeStruct(lead + (count, in_dev, wide), jnp.bfloat16))
            zero = (0,) * (len(lead) + 1)
            specs.append(
                pl.BlockSpec(lead + (count, group, wide), lambda i, zero=zero: zero + (i, 0))
            )
    return pl.pallas_call(
        functools.partial(channelize_kernel, chunks, spectra_len),
        grid=(in_dev // group,),
        in_specs=[
            pl.BlockSpec((2, 1, group, samples), lambda i: (0, 0, i, 0)),
            pl.BlockSpec(taps.shape, lambda i: (0, 0)),
            pl.BlockSpec(table.shape, lambda i: (0, 0)),
        ],
        out_specs=specs,
        out_shape=shapes,
        scratch_shapes=[
            pltpu.VMEM((2 * points // LANES, 8 * spectra_len, LANES), jnp.float32),
            pltpu.VMEM((wide // LANES, chans * group, LANES), jnp.float32),
        ],
        compiler_params=pltpu.CompilerParams(vmem_limit_bytes=56 << 20),
        cost_estimate=pl.CostEstimate(
            flops=6 * in_dev * spectra_len * 2 * chans * 2 * points,
            bytes_accessed=voltages.size * 4 + in_dev * wide * chans * 2,
            transcendentals=0,
        ),
    )(voltages, taps, table)


ROLES = ("own", "d1", "ua3", "d2", "u2", "xa_own", "xa_n2", "xb12", "xb3")


def role_used(role, z, x):
    return {
        "own": 1,
        "d1": jnp.where(z < 3, 1, 0),
        "ua3": jnp.where(z == 3, 1, 0),
        "d2": jnp.where(z < 2, 1, 0),
        "u2": jnp.where(z >= 2, 1, 0),
        "xa_own": 1 - x,
        "xa_n2": x,
        "xb12": jnp.where(z < 3, 1, 0),
        "xb3": jnp.where(z == 3, 1, 0),
    }[role]


def correlate_kernel(scale, aliased, info_ref, *refs):
    n_in = 2 * len(ROLES)
    halves = [dict(zip(ROLES, refs[h * len(ROLES) : (h + 1) * len(ROLES)])) for h in range(2)]
    out_ref, block_ref, left_ref = refs[n_in + (1 if aliased else 0) :]
    f, z, x = info_ref[0], info_ref[1], info_ref[2]
    rows = halves[0]["own"].shape[1] // 2
    wide = halves[0]["own"].shape[2]
    half_wide = wide // 2

    def place(slot, role):
        for h in range(2):
            for sub in range(2):
                at = pl.multiple_of((f ^ (2 * h + sub)) * rows, rows)
                block_ref[slot, pl.ds(at, rows), :] = halves[h][role][
                    0, sub * rows : (sub + 1) * rows, :
                ]

    place(0, "own")

    @pl.when(x == 0)
    def _():
        place(1, "xa_own")

    @pl.when(x == 1)
    def _():
        place(3, "xa_n2")

    @pl.when(z < 3)
    def _():
        place(2, "d1")
        place(3 - 2 * x, "xb12")

    @pl.when(z == 3)
    def _():
        place(2, "ua3")
        place(3 - 2 * x, "xb3")

    @pl.when(z < 2)
    def _():
        place(4, "d2")

    @pl.when(z >= 2)
    def _():
        place(4, "u2")

    own = block_ref[0].astype(jnp.float32)
    size = own.shape[0]
    turned = jnp.concatenate([own[:, half_wide:], -own[:, :half_wide]], axis=1)
    for part in range(wide // LANES):
        cut = slice(part * LANES, (part + 1) * LANES)
        left_ref[part, pl.ds(0, size, stride=2), :] = own[:, cut]
        left_ref[part, pl.ds(1, size, stride=2), :] = turned[:, cut]
    left = jnp.concatenate(
        [left_ref[part].astype(jnp.bfloat16) for part in range(wide // LANES)], axis=1
    )
    for slot in range(5):
        product = lax.dot_general(
            left, block_ref[slot], ROWS_EACH, preferred_element_type=jnp.float32
        )
        out_ref[0, 0, slot] = (product * scale).astype(jnp.bfloat16).reshape(size, 2, size)


def correlate(info, first, second, out, start, out_shape):
    count, double_rows, wide = first["own"].shape
    size = 2 * double_rows

    def spec(role):
        return pl.BlockSpec(
            (1, double_rows, wide),
            lambda c, info_ref: (c * role_used(role, info_ref[1], info_ref[2]), 0, 0),
        )

    operands = [half[role] for half in (first, second) for role in ROLES]
    in_specs = [spec(role) for _ in range(2) for role in ROLES]
    aliased = out is not None
    aliases = {}
    if aliased:
        aliases = {1 + len(operands): 0}
        operands.append(out)
        in_specs.append(pl.BlockSpec(memory_space=pl.ANY))
    offsets = out_shape.shape[2]
    return pl.pallas_call(
        functools.partial(correlate_kernel, 2.0 / wide, aliased),
        grid_spec=pltpu.PrefetchScalarGridSpec(
            num_scalar_prefetch=1,
            grid=(count,),
            in_specs=in_specs,
            out_specs=pl.BlockSpec(
                (1, 1, offsets, size, 2, size),
                lambda c, info_ref: (c + start, 0, 0, 0, 0, 0),
            ),
            scratch_shapes=[
                pltpu.VMEM((offsets, size, wide), jnp.bfloat16),
                pltpu.VMEM((wide // LANES, 2 * size, LANES), jnp.float32),
            ],
        ),
        out_shape=out_shape,
        input_output_aliases=aliases,
        compiler_params=pltpu.CompilerParams(vmem_limit_bytes=40 << 20),
        cost_estimate=pl.CostEstimate(
            flops=2 * count * offsets * 2 * size * size * wide,
            bytes_accessed=count * offsets * size * (2 * size + wide) * 2,
            transcendentals=0,
        ),
    )(info, *operands)


def at(z, x):
    return 2 * z + x


DOWN = [(at(z + 1, x), at(z, x)) for z in range(3) for x in range(2)]
DOWN_AGAIN = [(at(z + 1, x), at(z, x)) for z in range(2) for x in range(2)]
UP_OWN = [(at(z, x), at(z + 1, x)) for z in range(2) for x in range(2)]
UP_AGAIN = [(at(z, x), at(z + 1, x)) for z in (1, 2) for x in range(2)]
UP_LAST = [(at(2, x), at(3, x)) for x in range(2)]
SIDE_OWN = [(at(z, 1), at(z, 0)) for z in range(4)]
SIDE_FAR = [(at(z, 0), at(z, 1)) for z in range(4)]
SIDE_NEXT = [(at(z, x), at(z, 1 - x)) for z in range(3) for x in range(2)]
SIDE_LAST = [(at(3, 0), at(3, 1)), (at(3, 1), at(3, 0))]


def sent(value, pairs):
    return lax.ppermute(value, "tri", pairs)


def behind(value, *others):
    return lax.optimization_barrier((value,) + others)[0]


def spread(units, z, x):
    got = []
    for index in range(len(units) + 1):
        last = got[index - 1] if index else None
        if index == len(units):
            far = jnp.where(z < 2, last["d2"], last["u2"])
            last["ua3"] = sent(last["u2"], UP_LAST)
            last["xa_n2"] = sent(far, SIDE_FAR)
            last["xb3"] = sent(last["ua3"], SIDE_LAST)
            break
        now = {"own": units[index]}
        got.append(now)
        own = units[index]
        if last is None:
            up = sent(own, UP_OWN)
            now["xa_own"] = sent(own, SIDE_OWN)
        else:
            own = behind(own, last["d2"], last["u2"], last["xa_own"], last["xb12"])
            far = jnp.where(z < 2, last["d2"], last["u2"])
            if last["own"].shape == own.shape:
                up = sent(jnp.where(z == 2, last["u2"], own), UP_OWN + UP_LAST)
                last["ua3"] = up
                now["xa_own"] = last["xa_n2"] = sent(jnp.where(x == 1, own, far), SIDE_OWN + SIDE_FAR)
            else:
                up = sent(own, UP_OWN)
                last["ua3"] = sent(last["u2"], UP_LAST)
                now["xa_own"] = sent(own, SIDE_OWN)
                last["xa_n2"] = sent(far, SIDE_FAR)
        now["d1"] = sent(own, DOWN)
        now["d2"] = sent(now["d1"], DOWN_AGAIN)
        now["u2"] = sent(up, UP_AGAIN)
        if last is not None and last["own"].shape == own.shape:
            now["xb12"] = last["xb3"] = sent(
                jnp.where(z == 3, up, now["d1"]), SIDE_NEXT + SIDE_LAST
            )
        else:
            now["xb12"] = sent(now["d1"], SIDE_NEXT)
            if last is not None:
                last["xb3"] = sent(last["ua3"], SIDE_LAST)
    return got


def on_device(voltages, window_taps):
    taps_count, points = window_taps.shape
    in_dev = voltages.shape[2]
    groups = lax.axis_size("freq")
    group_chans = CHAN // groups
    f = lax.axis_index("freq")
    t = lax.axis_index("tri")
    z, x = t // 2, t % 2
    info = jnp.stack([f, z, x]).astype(jnp.int32)

    exact = table_rows(points, CHAN)
    high = exact.astype(jnp.bfloat16)
    low = (exact - high.astype(np.float32)).astype(jnp.bfloat16)
    table = jnp.asarray(np.stack([high, low], 0)).reshape(2, 2, groups, group_chans, 2 * points)
    table = jnp.take(table, f ^ jnp.arange(groups), axis=2).reshape(4 * CHAN, 2 * points)

    pieces = channelize(voltages, window_taps, table, CHUNKS)
    chunk_count = len(CHUNKS)
    other_core = [(g, g ^ 1) for g in range(groups)]
    other_chip = [(g, g ^ 2) for g in range(groups)]
    near_units, far_units = [], []
    for k in range(chunk_count):
        near, across, paired = pieces[3 * k : 3 * k + 3]
        received = lax.ppermute(paired, "freq", other_core)
        near_units.append(jnp.concatenate([near, received[0]], axis=1))
        joined = jnp.concatenate([across, received[1]], axis=1)
        far_units.append(lax.ppermute(joined, "freq", other_chip))

    got = spread(near_units + far_units, z, x)
    block = in_dev * groups
    offsets = lax.axis_size("tri") // 2 + 1
    out_shape = jax.ShapeDtypeStruct((group_chans, 1, offsets, block, 2, block), jnp.bfloat16)
    out, start = None, 0
    for k in range(chunk_count):
        out = correlate(info, got[k], got[chunk_count + k], out, start, out_shape)
        start += CHUNKS[k]
    return out


def solution(mesh):
    placed = (P(None, "tri", "freq", None), P())
    small = mesh.shape["freq"] == 4 and mesh.shape["tri"] == 8
    return jax.shard_map(
        on_device if small else on_device_any,
        mesh=mesh,
        in_specs=placed,
        out_specs=P("freq", "tri", None, None, None, None),
        check_vma=False,
    )
```

```python
import functools
import math

import jax
import jax.numpy as jnp
import numpy as np
from jax import lax
from jax.experimental import pallas as pl
from jax.experimental.pallas import tpu as pltpu
from jax.sharding import PartitionSpec as P

CHAN = 128


spectrum_scale = 1.0 / 128.0

LANES = 128
CHUNKS = (4,) * 8
STREAMS = 2
LEAD = 2
DELAY = 100
ROWS_EACH = ((((1,), (1,)), ((), ())))


def passed_along(value, axis, steps):
    count = lax.axis_size(axis)
    pairs = [(source, (source + steps) % count) for source in range(count)]
    return lax.ppermute(value, axis, pairs)


def fourier_table(points, chans):
    point_index = jnp.arange(points, dtype=jnp.int32)[:, None]
    chan_index = jnp.arange(chans, dtype=jnp.int32)[None, :]
    phase = (point_index * chan_index % points).astype(jnp.float32) * (2.0 * math.pi / points)
    cosine = jnp.cos(phase)
    sine = jnp.sin(phase)
    table = jnp.stack([jnp.stack([cosine, -sine], -1), jnp.stack([sine, cosine], -1)], 0)
    return table * spectrum_scale


def fir_frames(samples, window_taps, count):
    frames = samples[:, :, 0:count, :] * window_taps[0]
    for tap_index in range(1, window_taps.shape[0]):
        frames = frames + samples[:, :, tap_index : tap_index + count, :] * window_taps[tap_index]
    return frames


def cross_tile(left_rows, right_block):
    spectra_len = right_block.shape[-1]
    real_part = right_block[..., 0, :]
    imag_part = right_block[..., 1, :]
    stacked = jnp.stack(
        [jnp.concatenate([real_part, imag_part], -1), jnp.concatenate([-imag_part, real_part], -1)],
        axis=-3,
    )
    product = jnp.einsum(
        "...at,...nbt->...anb", left_rows, stacked, preferred_element_type=jnp.float32
    )
    return (product * (1.0 / spectra_len)).astype(jnp.bfloat16)


def on_device_any(voltages, window_taps):
    taps_count, points = window_taps.shape
    in_dev = voltages.shape[2]
    frames_total = voltages.shape[3] // points
    spectra_len = frames_total - taps_count + 1
    samples = voltages.reshape(2, in_dev, frames_total, points).astype(jnp.float32)
    frames = fir_frames(samples, window_taps, spectra_len)
    spectra = jnp.einsum(
        "qpcr,qimp->cirm", fourier_table(points, CHAN), frames, precision=lax.Precision.HIGHEST
    ).astype(jnp.bfloat16)
    half_count = lax.axis_size("tri") // 2
    own_block = lax.all_to_all(spectra, "freq", split_axis=0, concat_axis=1, tiled=True)
    group_chans, block_len = own_block.shape[:2]
    left_rows = own_block.reshape(group_chans, block_len, 2 * spectra_len)
    held = own_block[None]
    while held.shape[0] < half_count + 1:
        run_len = held.shape[0]
        count = min(run_len, half_count + 1 - run_len)
        received = passed_along(held[:count], "tri", -run_len)
        held = jnp.concatenate([held, received], 0)
    tile_list = [cross_tile(left_rows, held[offset]) for offset in range(half_count + 1)]
    return jnp.stack(tile_list, axis=1)[:, None]


def table_rows(points, chans):
    phase = (np.arange(points)[:, None] * np.arange(chans)[None, :] % points).astype(np.float64)
    phase = phase * (2.0 * math.pi / points)
    cosine, sine = np.cos(phase), np.sin(phase)
    real_row = np.concatenate([cosine, sine], 0).T
    imag_row = np.concatenate([-sine, cosine], 0).T
    return (np.stack([real_row, imag_row], 0) * spectrum_scale).astype(np.float32)


def channelize_kernel(chunks, spectra_len, volt_ref, taps_ref, table_ref, *refs):
    n_out = 3 * len(chunks)
    outs = refs[:n_out]
    frames_ref, spec_ref = refs[n_out:]
    points = taps_ref.shape[1]
    taps_count = taps_ref.shape[0] // 8
    lane_parts = points // LANES
    group = volt_ref.shape[2]
    total_chans = table_ref.shape[0] // 4
    n_rows = 2 * total_chans

    for sub in range(group // 8):
        weight = [
            [
                taps_ref[8 * k : 8 * k + 8, part * LANES : (part + 1) * LANES]
                for k in range(taps_count)
            ]
            for part in range(lane_parts)
        ]

        def sample(m, q, part, sub=sub):
            start = pl.multiple_of(m * points + part * LANES, LANES)
            return volt_ref[q, 0, 8 * sub : 8 * sub + 8, pl.ds(start, LANES)].astype(jnp.float32)

        step = 8

        def body(i, carry, weight=weight, sample=sample):
            held = [list(c) for c in carry]
            for r in range(step):
                m = i * step + r
                row = pl.multiple_of(m * 8, 8)
                for q in range(2):
                    for part in range(lane_parts):
                        which = q * lane_parts + part
                        now = held[which] + [sample(m + taps_count - 1, q, part)]
                        total = now[0] * weight[part][0]
                        for k in range(1, taps_count):
                            total = total + now[k] * weight[part][k]
                        held[which] = now[1:]
                        frames_ref[which, pl.ds(row, 8), :] = total
            return tuple(tuple(h) for h in held)

        first_samples = tuple(
            tuple(sample(k, q, part) for k in range(taps_count - 1))
            for q in range(2)
            for part in range(lane_parts)
        )
        lax.fori_loop(0, spectra_len // step, body, first_samples)

        def one_input(n, carry, sub=sub):
            frame = jnp.concatenate(
                [
                    frames_ref[part, pl.ds(n, spectra_len, stride=8), :]
                    for part in range(2 * lane_parts)
                ],
                axis=1,
            )
            high = frame.astype(jnp.bfloat16)
            low = (frame - high.astype(jnp.float32)).astype(jnp.bfloat16)
            first = lax.dot_general(
                table_ref[0 : 2 * n_rows, :], high, ROWS_EACH, preferred_element_type=jnp.float32
            )
            second = lax.dot_general(
                table_ref[0:n_rows, :], low, ROWS_EACH, preferred_element_type=jnp.float32
            )
            spec = first[:n_rows] + (first[n_rows:] + second)
            for ri in range(2):
                for part in range(spectra_len // LANES):
                    spec_ref[
                        ri * (spectra_len // LANES) + part,
                        pl.ds(sub * 8 + n, total_chans, stride=group),
                        :,
                    ] = spec[
                        ri * total_chans : (ri + 1) * total_chans, part * LANES : (part + 1) * LANES
                    ]
            return carry

        lax.fori_loop(0, 8, one_input, 0, unroll=True)

    group_chans = sum(chunks)
    n_parts = 2 * spectra_len // LANES
    start = 0
    for k, count in enumerate(chunks):
        near, across, paired = outs[3 * k : 3 * k + 3]
        for j, target in ((0, near), (2, across), (1, paired.at[0]), (3, paired.at[1])):
            base = (j * group_chans + start) * group
            for part in range(n_parts):
                piece = spec_ref[part, base : base + count * group, :].astype(jnp.bfloat16)
                target[:, :, part * LANES : (part + 1) * LANES] = piece.reshape(count, group, LANES)
        start += count


def channelize(voltages, window_taps, table, chunks):
    taps_count, points = window_taps.shape
    in_dev, samples = voltages.shape[2:]
    spectra_len = samples // points - taps_count + 1
    group = 16
    wide = 2 * spectra_len
    chans = table.shape[0] // 4
    taps = jnp.repeat(window_taps, 8, axis=0)
    shapes, specs = [], []
    for count in chunks:
        for lead in ((), (), (2,)):
            shapes.append(jax.ShapeDtypeStruct(lead + (count, in_dev, wide), jnp.bfloat16))
            zero = (0,) * (len(lead) + 1)
            specs.append(
                pl.BlockSpec(lead + (count, group, wide), lambda i, zero=zero: zero + (i, 0))
            )
    return pl.pallas_call(
        functools.partial(channelize_kernel, chunks, spectra_len),
        grid=(in_dev // group,),
        in_specs=[
            pl.BlockSpec((2, 1, group, samples), lambda i: (0, 0, i, 0)),
            pl.BlockSpec(taps.shape, lambda i: (0, 0)),
            pl.BlockSpec(table.shape, lambda i: (0, 0)),
        ],
        out_specs=specs,
        out_shape=shapes,
        scratch_shapes=[
            pltpu.VMEM((2 * points // LANES, 8 * spectra_len, LANES), jnp.float32),
            pltpu.VMEM((wide // LANES, chans * group, LANES), jnp.float32),
        ],
        compiler_params=pltpu.CompilerParams(vmem_limit_bytes=56 << 20),
        cost_estimate=pl.CostEstimate(
            flops=6 * in_dev * spectra_len * 2 * chans * 2 * points,
            bytes_accessed=voltages.size * 4 + in_dev * wide * chans * 2,
            transcendentals=0,
        ),
    )(voltages, taps, table)


ROLES = ("own", "d1", "ua3", "d2", "u2", "xa_own", "xa_n2", "xb12", "xb3")


def role_used(role, z, x):
    return {
        "own": 1,
        "d1": jnp.where(z < 3, 1, 0),
        "ua3": jnp.where(z == 3, 1, 0),
        "d2": jnp.where(z < 2, 1, 0),
        "u2": jnp.where(z >= 2, 1, 0),
        "xa_own": 1 - x,
        "xa_n2": x,
        "xb12": jnp.where(z < 3, 1, 0),
        "xb3": jnp.where(z == 3, 1, 0),
    }[role]


def correlate_kernel(scale, aliased, info_ref, *refs):
    n_in = 2 * len(ROLES)
    halves = [dict(zip(ROLES, refs[h * len(ROLES) : (h + 1) * len(ROLES)])) for h in range(2)]
    out_ref, token_ref, block_ref, left_ref = refs[n_in + (1 if aliased else 0) :]
    token_ref[...] = jnp.zeros_like(token_ref)
    f, z, x = info_ref[0], info_ref[1], info_ref[2]
    rows = halves[0]["own"].shape[1] // 2
    wide = halves[0]["own"].shape[2]
    half_wide = wide // 2

    def place(slot, role):
        for h in range(2):
            for sub in range(2):
                at = pl.multiple_of((f ^ (2 * h + sub)) * rows, rows)
                block_ref[slot, pl.ds(at, rows), :] = halves[h][role][
                    0, sub * rows : (sub + 1) * rows, :
                ]

    place(0, "own")

    @pl.when(x == 0)
    def _():
        place(1, "xa_own")

    @pl.when(x == 1)
    def _():
        place(3, "xa_n2")

    @pl.when(z < 3)
    def _():
        place(2, "d1")
        place(3 - 2 * x, "xb12")

    @pl.when(z == 3)
    def _():
        place(2, "ua3")
        place(3 - 2 * x, "xb3")

    @pl.when(z < 2)
    def _():
        place(4, "d2")

    @pl.when(z >= 2)
    def _():
        place(4, "u2")

    own = block_ref[0].astype(jnp.float32)
    size = own.shape[0]
    turned = jnp.concatenate([own[:, half_wide:], -own[:, :half_wide]], axis=1)
    for part in range(wide // LANES):
        cut = slice(part * LANES, (part + 1) * LANES)
        left_ref[part, pl.ds(0, size, stride=2), :] = own[:, cut]
        left_ref[part, pl.ds(1, size, stride=2), :] = turned[:, cut]
    left = jnp.concatenate(
        [left_ref[part].astype(jnp.bfloat16) for part in range(wide // LANES)], axis=1
    )
    for slot in range(5):
        product = lax.dot_general(
            left, block_ref[slot], ROWS_EACH, preferred_element_type=jnp.float32
        )
        out_ref[0, 0, slot] = (product * scale).astype(jnp.bfloat16).reshape(size, 2, size)


def correlate(info, first, second, out, start, out_shape):
    count, double_rows, wide = first["own"].shape
    size = 2 * double_rows

    def spec(role):
        return pl.BlockSpec(
            (1, double_rows, wide),
            lambda c, info_ref: (c * role_used(role, info_ref[1], info_ref[2]), 0, 0),
        )

    operands = [half[role] for half in (first, second) for role in ROLES]
    in_specs = [spec(role) for _ in range(2) for role in ROLES]
    aliased = out is not None
    aliases = {}
    if aliased:
        aliases = {1 + len(operands): 0}
        operands.append(out)
        in_specs.append(pl.BlockSpec(memory_space=pl.ANY))
    offsets = out_shape.shape[2]
    return pl.pallas_call(
        functools.partial(correlate_kernel, 2.0 / wide, aliased),
        grid_spec=pltpu.PrefetchScalarGridSpec(
            num_scalar_prefetch=1,
            grid=(count,),
            in_specs=in_specs,
            out_specs=[
                pl.BlockSpec(
                    (1, 1, offsets, size, 2, size),
                    lambda c, info_ref: (c + start, 0, 0, 0, 0, 0),
                ),
                pl.BlockSpec((8, LANES), lambda c, info_ref: (0, 0)),
            ],
            scratch_shapes=[
                pltpu.VMEM((offsets, size, wide), jnp.bfloat16),
                pltpu.VMEM((wide // LANES, 2 * size, LANES), jnp.float32),
            ],
        ),
        out_shape=[out_shape, jax.ShapeDtypeStruct((8, LANES), jnp.int32)],
        input_output_aliases=aliases,
        compiler_params=pltpu.CompilerParams(vmem_limit_bytes=60 << 20),
        cost_estimate=pl.CostEstimate(
            flops=2 * count * offsets * 2 * size * size * wide,
            bytes_accessed=count * offsets * size * (2 * size + wide) * 2,
            transcendentals=0,
        ),
    )(info, *operands)


def at(z, x):
    return 2 * z + x


DOWN = [(at(z + 1, x), at(z, x)) for z in range(3) for x in range(2)]
DOWN_AGAIN = [(at(z + 1, x), at(z, x)) for z in range(2) for x in range(2)]
UP_OWN = [(at(z, x), at(z + 1, x)) for z in range(2) for x in range(2)]
UP_AGAIN = [(at(z, x), at(z + 1, x)) for z in (1, 2) for x in range(2)]
UP_LAST = [(at(2, x), at(3, x)) for x in range(2)]
SIDE_OWN = [(at(z, 1), at(z, 0)) for z in range(4)]
SIDE_FAR = [(at(z, 0), at(z, 1)) for z in range(4)]
SIDE_NEXT = [(at(z, x), at(z, 1 - x)) for z in range(3) for x in range(2)]
SIDE_LAST = [(at(3, 0), at(3, 1)), (at(3, 1), at(3, 0))]


def sent(value, pairs):
    return lax.ppermute(value, "tri", pairs)


def behind(value, *others):
    return lax.optimization_barrier((value,) + others)[0]


def spread(units, z, x, gate_on):
    got = []
    for index in range(len(units) + STREAMS):
        past = index - STREAMS
        last = got[past] if past >= 0 else None
        if last is not None:
            far = jnp.where(z < 2, last["d2"], last["u2"])
        if index >= len(units):
            last["ua3"] = sent(last["u2"], UP_LAST)
            last["xa_n2"] = sent(far, SIDE_FAR)
            last["xb3"] = sent(behind(last["ua3"], last["xa_n2"]), SIDE_LAST)
            continue
        own = units[index]
        now = {"own": own}
        got.append(now)
        if last is None:
            up = sent(own, UP_OWN)
            now["xa_own"] = sent(own, SIDE_OWN)
        else:
            own = behind(own, last["d2"], last["u2"], last["xa_own"], last["xb12"])
            late = gate_on(index, got)
            up = last["ua3"] = sent(jnp.where(z + late == 2, last["u2"], own), UP_OWN + UP_LAST)
            now["xa_own"] = last["xa_n2"] = sent(
                jnp.where(x + late == 1, own, far), SIDE_OWN + SIDE_FAR
            )
        now["d1"] = sent(own, DOWN)
        down = now["d1"]
        if index >= len(units) - STREAMS:
            down = behind(down, up, now["xa_own"])
        now["d2"] = sent(down, DOWN_AGAIN)
        now["u2"] = sent(up, UP_AGAIN)
        if last is None:
            now["xb12"] = sent(now["d1"], SIDE_NEXT)
        else:
            now["xb12"] = last["xb3"] = sent(
                jnp.where(z == 3, up, now["d1"]), SIDE_NEXT + SIDE_LAST
            )
    return got


def on_device(voltages, window_taps):
    taps_count, points = window_taps.shape
    in_dev = voltages.shape[2]
    groups = lax.axis_size("freq")
    group_chans = CHAN // groups
    f = lax.axis_index("freq")
    t = lax.axis_index("tri")
    z, x = t // 2, t % 2
    info = jnp.stack([f, z, x]).astype(jnp.int32)

    exact = table_rows(points, CHAN)
    high = exact.astype(jnp.bfloat16)
    low = (exact - high.astype(np.float32)).astype(jnp.bfloat16)
    table = jnp.asarray(np.stack([high, low], 0)).reshape(2, 2, groups, group_chans, 2 * points)
    table = jnp.take(table, f ^ jnp.arange(groups), axis=2).reshape(4 * CHAN, 2 * points)

    pieces = channelize(voltages, window_taps, table, CHUNKS)
    chunk_count = len(CHUNKS)
    other_core = [(g, g ^ 1) for g in range(groups)]
    other_chip = [(g, g ^ 2) for g in range(groups)]
    near_units, far_units = [], []
    for k in range(chunk_count):
        near, across, paired = pieces[3 * k : 3 * k + 3]
        received = lax.ppermute(paired, "freq", other_core)
        near_units.append(jnp.concatenate([near, received[0]], axis=1))
        joined = jnp.concatenate([across, received[1]], axis=1)
        far_units.append(lax.ppermute(joined, "freq", other_chip))

    order = [(0, k) for k in range(LEAD)]
    for k in range(chunk_count):
        order += [(1, k)] + ([(0, k + LEAD)] if k + LEAD < chunk_count else [])
    place = {unit: index for index, unit in enumerate(order)}
    block = in_dev * groups
    offsets = lax.axis_size("tri") // 2 + 1
    out_shape = jax.ShapeDtypeStruct((group_chans, 1, offsets, block, 2, block), jnp.bfloat16)
    state = {"out": None, "next": 0}

    def correlate_next(got):
        k = state["next"]
        state["out"], token = correlate(
            info, got[place[0, k]], got[place[1, k]], state["out"], sum(CHUNKS[:k]), out_shape
        )
        state["next"] = k + 1
        return token

    def gate_on(index, got):
        token = jnp.int32(0)
        while state["next"] < chunk_count and place[1, state["next"]] + DELAY <= index:
            token = correlate_next(got)[0, 0]
        return token

    got = spread([(near_units, far_units)[h][k] for h, k in order], z, x, gate_on)
    while state["next"] < chunk_count:
        correlate_next(got)
    return state["out"]


def solution(mesh):
    placed = (P(None, "tri", "freq", None), P())
    small = mesh.shape["freq"] == 4 and mesh.shape["tri"] == 8
    return jax.shard_map(
        on_device if small else on_device_any,
        mesh=mesh,
        in_specs=placed,
        out_specs=P("freq", "tri", None, None, None, None),
        check_vma=False,
    )
```
